512 devices in a mesh: head: 8 (over y), ctx: 64 (over x, z, core).
Axes of the slice: x: 4, y: 8, z: 8, core: 2. Of those that a mesh axis runs over, the one named last changes fastest.
Arguments:
- queries: bfloat16 [32768, 1024], P('ctx', 'head'), may hold values from -40 to 40
- keys: bfloat16 [32768, 128], P('ctx'), may hold values from -5 to 5
- values: bfloat16 [32768, 128], P('ctx'), may hold values from -6 to 6
- d_out: bfloat16 [64, 512, 1024], P('ctx', 'head'), may hold values from -6 to 6
- lengths: int32 [64], replicated, may hold values from 1 to 1024, 32768 in all
Outputs:
- grad_queries: bfloat16 [32768, 1024], P('ctx', 'head')
- grad_keys: bfloat16 [64, 512, 128], P('ctx', 'head')
- grad_values: bfloat16 [64, 512, 128], P('ctx', 'head')
The draws below stay inside these ranges and needn't reach their ends.
Inputs may be any that keep to these rules, and one draw needn't show every extreme that they name: `lengths`: 64 documents that fill the 32768 tokens exactly; the longest has exactly 1024 tokens.
All inputs are finite; a program needn't handle non-finite values.
Results may differ from the reference program's by a relative error of at most 0.0055.
Values may be sent and summed in bfloat16 or wider, within the bound.
No kernel may reach another device: no remote copies, remote signals or barrier semaphores. Data moves between devices by JAX's collectives and lax.ppermute only.
A program may use at most 64 MiB of HBM per device.

```python
import math
import jax
import jax.numpy as jnp
import numpy as np
from jax import lax

HQ = 8
DH = 128
TOK_DEV = 512
SPAN = 2
SHARDS = 64
TOKENS = 32768
DOCS = 64
MOST = 1024


def shared_draw(key):
    base = jax.random.fold_in(key, 29)
    first, second = jax.random.split(base)
    key_rows = jnp.clip(jax.random.normal(first, (TOKENS, DH), jnp.float32), -5.0, 5.0)
    query_rows = jnp.clip(jax.random.normal(second, (TOKENS, HQ * DH), jnp.float32), -5.0, 5.0)
    return (query_rows, key_rows)


def draw_queries(key, part):
    return shared_draw(key)[0].astype(jnp.bfloat16)


def draw_keys(key, part):
    return shared_draw(key)[1].astype(jnp.bfloat16)


def level_of(own_key, shape, shards, low, top_value):
    factor_of, own = 1.0, jax.random.fold_in(own_key, 6)
    for dim, shards_of in shards:
        draws = jnp.exp(jax.random.uniform(jax.random.fold_in(own, dim), (shards_of,), jnp.float32, low / len(shards), top_value / len(shards)))
        factor_of = factor_of * jnp.repeat(draws, shape[dim] // shards_of).reshape([-1 if axis == dim else 1 for axis in range(len(shape))])
    return factor_of


def length_profile(count, total, reach, slope):
    loads = [(1 << 20) // math.isqrt(standing ** slope) + 1 for standing in range(2, count + 1)]
    spare, given = total - reach - (count - 1), [1] * (count - 1)
    while spare > 0:
        candidates = [i for i in range(count - 1) if given[i] < reach]
        pool, budget = sum([loads[i] for i in candidates]), spare
        for i in candidates:
            addition = min(reach - given[i], max(1, budget * loads[i] // pool), spare)
            given[i] = given[i] + addition
            spare = spare - addition
    return np.array([reach] + given)


def ragged_sizes(rng, count, total, bound, lean):
    if count == 2:
        one = jax.random.randint(rng, (), max(1, total - bound), min(bound, total - 1) + 1)
        return jnp.stack([one, total - one])
    sizes = jnp.asarray(length_profile(count, total, bound, lean), jnp.int32)
    couples = (count - 1) // 2
    giver, taker = sizes[1:1 + 2 * couples:2], sizes[2:2 + 2 * couples:2]
    margin = jnp.minimum(giver - 1, bound - taker)
    passed = jax.random.randint(jax.random.fold_in(rng, 1), (couples,), 0, 1 << 20) % (margin + 1)
    sizes = sizes.at[1:1 + 2 * couples:2].set(giver - passed).at[2:2 + 2 * couples:2].set(taker + passed)
    return sizes[jax.random.permutation(jax.random.fold_in(rng, 2), count)]


def bell_draw(own_key, shape, deviation, bound, pieces=(), kind=jnp.bfloat16):
    values = jax.random.normal(own_key, shape, jnp.float32) * deviation
    if len(pieces) > 0:
        values = level_of(own_key, shape, pieces, -0.22, 0.18) * values
    return jnp.clip(values, min=-bound, max=bound).astype(kind)


def setup_inputs(seed: int = 0) -> dict:
    seeds = jax.random.split(jax.random.key(seed), 6)
    return {
        "queries": draw_queries(jax.random.fold_in(seeds[5], 71), 0),
        "keys": draw_keys(jax.random.fold_in(seeds[5], 71), 0),
        "values": bell_draw(seeds[2], (TOKENS, DH), 1.0, 6.0, ((0, 64),)),
        "d_out": bell_draw(seeds[3], (SHARDS, TOK_DEV, HQ * DH), 1.0, 6.0, ((0, 64), (1, 8))),
        "lengths": ragged_sizes(seeds[4], DOCS, TOKENS, MOST, 2).astype(jnp.int32),
    }


def reference(queries, keys, values, d_out, lengths):
    blocks = TOKENS // TOK_DEV
    width = (SPAN + 1) * TOK_DEV
    scale = DH ** -0.5
    query_blocks = queries.reshape(blocks, TOK_DEV, HQ, DH)
    grad_blocks = d_out.reshape(blocks, TOK_DEV, HQ, DH)
    padding = jnp.zeros((SPAN * TOK_DEV, DH), jnp.bfloat16)
    keys_padded = jnp.concatenate([padding, keys], axis=0)
    values_padded = jnp.concatenate([padding, values], axis=0)
    lengths32 = lengths.astype(jnp.int32)
    starts = (jnp.cumsum(lengths32) - lengths32).astype(jnp.int32)
    offsets = jnp.arange(TOK_DEV, dtype=jnp.int32)
    window_offsets = jnp.arange(width, dtype=jnp.int32)

    def one_block(carry, inputs):
        key_grads, value_grads = carry
        query_block, grad_block, index = inputs
        first = (index * TOK_DEV).astype(jnp.int32)
        key_window = lax.dynamic_slice_in_dim(keys_padded, first, width, 0).astype(jnp.float32)
        value_window = lax.dynamic_slice_in_dim(values_padded, first, width, 0).astype(jnp.float32)
        query_pos = first + offsets
        key_pos = first - SPAN * TOK_DEV + window_offsets
        query_start = jnp.max(jnp.where(starts[None, :] <= query_pos[:, None], starts[None, :], 0), axis=1)
        visible = (key_pos[None, :] <= query_pos[:, None]) & (key_pos[None, :] >= query_start[:, None])
        query_f = query_block.astype(jnp.float32)
        grad_f = grad_block.astype(jnp.float32)
        scores = jnp.einsum("thd,kd->htk", query_f, key_window) * scale
        scores = jnp.where(visible[None], scores, -1e30)
        highest = jnp.max(scores, axis=2)
        log_total = highest + jnp.log(jnp.sum(jnp.exp(scores - highest[:, :, None]), axis=2))
        probs = jnp.exp(scores - log_total[:, :, None])
        weights = probs.astype(jnp.bfloat16).astype(jnp.float32)
        attended = jnp.einsum("htk,kd->thd", weights, value_window)
        delta = jnp.sum(grad_f * attended, axis=2)
        dprobs = jnp.einsum("thd,kd->htk", grad_f, value_window)
        dscores = (probs * (dprobs - delta.T[:, :, None])).astype(jnp.bfloat16).astype(jnp.float32)
        grad_query = jnp.einsum("htk,kd->thd", dscores, key_window) * scale
        key_term = jnp.einsum("htk,thd->kd", dscores, query_f) * scale
        value_term = jnp.einsum("htk,thd->kd", weights, grad_f)
        old_keys = lax.dynamic_slice_in_dim(key_grads, first, width, 0)
        old_values = lax.dynamic_slice_in_dim(value_grads, first, width, 0)
        key_grads = lax.dynamic_update_slice_in_dim(key_grads, old_keys + key_term, first, 0)
        value_grads = lax.dynamic_update_slice_in_dim(value_grads, old_values + value_term, first, 0)
        return (key_grads, value_grads), grad_query.astype(jnp.bfloat16).reshape(TOK_DEV, HQ * DH)

    start_carry = (jnp.zeros((TOKENS + SPAN * TOK_DEV, DH), jnp.float32), jnp.zeros((TOKENS + SPAN * TOK_DEV, DH), jnp.float32))
    indices = jnp.arange(blocks, dtype=jnp.int32)
    final, grad_rows = lax.scan(one_block, start_carry, (query_blocks, grad_blocks, indices))
    grad_queries = grad_rows.reshape(TOKENS, HQ * DH)
    grad_keys = final[0][SPAN * TOK_DEV:].astype(jnp.bfloat16).reshape(blocks, TOK_DEV, DH)
    grad_values = final[1][SPAN * TOK_DEV:].astype(jnp.bfloat16).reshape(blocks, TOK_DEV, DH)
    return (grad_queries, grad_keys, grad_values)
```

```python
import functools

import jax
import jax.numpy as jnp
from jax import lax
from jax.experimental import pallas as pl
from jax.experimental.pallas import tpu as pltpu
from jax.sharding import PartitionSpec as P

DH = 128
SPAN = 2
LOG2E = 1.4426950408889634


def shifted(value, axis, steps):
    count = lax.axis_size(axis)
    leading, last = (max(0, -steps), min(count, count - steps))
    return lax.ppermute(value, axis, [(source, source + steps) for source in range(leading, last)])


def nt(a, b):
    return lax.dot_general(a, b, (((1,), (1,)), ((), ())), preferred_element_type=jnp.float32)


def nn(a, b):
    return lax.dot_general(a, b, (((1,), (0,)), ((), ())), preferred_element_type=jnp.float32)


def attention_kernel(shard_ref, len_row_ref, len_col_ref, q_ref, do_ref, kv0_ref, kv1_ref, kv2_ref,
                     dq_ref, own_ref, one_ref, two_ref):
    rows = q_ref.shape[0]
    scale = DH ** (-0.5)
    first = shard_ref[0] * rows
    docs = len_row_ref.shape[1]
    j = lax.broadcasted_iota(jnp.int32, (docs, docs), 0)
    k = lax.broadcasted_iota(jnp.int32, (docs, docs), 1)
    ends = jnp.sum(jnp.where(k <= j, len_row_ref[...], 0), axis=1, keepdims=True)
    query_pos = first + lax.broadcasted_iota(jnp.int32, (1, rows), 1)
    start = jnp.sum(jnp.where(ends <= query_pos, len_col_ref[...], 0), axis=0, keepdims=True)
    q = q_ref[...]
    do = do_ref[...]
    sub = lax.broadcasted_iota(jnp.int32, (rows, rows), 0)
    lane = lax.broadcasted_iota(jnp.int32, (rows, rows), 1)
    kvs = (kv0_ref, kv1_ref, kv2_ref)
    scores = []
    for distance in range(SPAN + 1):
        plain = nt(kvs[distance][:rows], q) * (scale * LOG2E)
        seen = sub >= start - (first - distance * rows)
        if distance == 0:
            seen = seen & (sub <= lane)
        scores.append(jnp.where(seen, plain, -1e30))
    highest = functools.reduce(jnp.maximum, [jnp.max(s, axis=0, keepdims=True) for s in scores])
    probs = [jnp.exp2(s - highest) for s in scores]
    total = functools.reduce(jnp.add, [jnp.sum(p, axis=0, keepdims=True) for p in probs])
    inverse = 1.0 / total
    probs = [p * inverse for p in probs]
    weights = [p.astype(jnp.bfloat16) for p in probs]
    dprobs = [nt(kv[rows:], do) for kv in kvs]
    delta = functools.reduce(
        jnp.add,
        [jnp.sum(w.astype(jnp.float32) * d, axis=0, keepdims=True) for w, d in zip(weights, dprobs)],
    )
    dscores = [(p * (d - delta)).astype(jnp.bfloat16) for p, d in zip(probs, dprobs)]
    for distance, out in enumerate((own_ref, one_ref, two_ref)):
        out[:rows] = (nn(dscores[distance], q) * scale).astype(out.dtype)
        out[rows:] = nn(weights[distance], do).astype(out.dtype)
    dq_t = functools.reduce(
        jnp.add, [nn(kv[:rows].T, d) for kv, d in zip(kvs, dscores)]
    )
    dq_ref[...] = (dq_t.T * scale).astype(dq_ref.dtype)


def attention(shard, lengths, q, do, kv0, kv1, kv2):
    rows = q.shape[0]
    docs = lengths.shape[0]
    vmem = pl.BlockSpec(memory_space=pltpu.VMEM)
    pair = (2 * rows, DH)
    return pl.pallas_call(
        attention_kernel,
        out_shape=(
            jax.ShapeDtypeStruct((rows, DH), jnp.bfloat16),
            jax.ShapeDtypeStruct(pair, jnp.float32),
            jax.ShapeDtypeStruct(pair, jnp.bfloat16),
            jax.ShapeDtypeStruct(pair, jnp.bfloat16),
        ),
        in_specs=[pl.BlockSpec(memory_space=pltpu.SMEM)] + [vmem] * 7,
        out_specs=(vmem,) * 4,
        compiler_params=pltpu.CompilerParams(vmem_limit_bytes=40 * 1024 * 1024),
        name="attention",
    )(shard, lengths.reshape(1, docs), lengths.reshape(docs, 1), q, do, kv0, kv1, kv2)


def shards(queries, keys, values, d_out, lengths):
    rows = keys.shape[0]
    heads = lax.axis_size("head")
    part = rows // heads
    kv = jnp.concatenate([keys, values], axis=0)
    behind = [shifted(kv, "ctx", distance) for distance in range(1, SPAN + 1)]
    by_head = d_out.reshape(part, heads, DH).transpose(1, 0, 2)
    do = lax.all_to_all(by_head, "head", split_axis=0, concat_axis=0, tiled=True).reshape(rows, DH)
    shard = lax.axis_index("ctx").astype(jnp.int32).reshape(1)
    grad_queries, own, one, two = attention(shard, lengths, queries, do, kv, *behind)
    two = shifted(two, "ctx", -2)
    one = shifted(one, "ctx", -1)
    total = (own + one.astype(jnp.float32) + two.astype(jnp.float32)).astype(jnp.bfloat16)
    total = total.reshape(2, heads, part, DH).transpose(1, 0, 2, 3)
    shares = lax.all_to_all(total, "head", split_axis=0, concat_axis=0, tiled=True)
    share = jnp.sum(shares.astype(jnp.float32), axis=0).astype(jnp.bfloat16)
    return (grad_queries, share[0][None], share[1][None])


def solution(mesh):
    in_specs = (P("ctx", "head"), P("ctx", None), P("ctx", None), P("ctx", "head", None), P())
    out_specs = (P("ctx", "head"), P("ctx", "head", None), P("ctx", "head", None))
    return jax.shard_map(shards, mesh=mesh, in_specs=in_specs, out_specs=out_specs, check_vma=False)
```

```python
import functools

import jax
import jax.numpy as jnp
from jax import lax
from jax.experimental import pallas as pl
from jax.experimental.pallas import tpu as pltpu
from jax.sharding import PartitionSpec as P

DH = 128
SPAN = 2
LOG2E = 1.4426950408889634
SCALE = DH ** (-0.5)
VMEM = pl.BlockSpec(memory_space=pltpu.VMEM)
SMEM = pl.BlockSpec(memory_space=pltpu.SMEM)


def shifted(value, axis, steps):
    count = lax.axis_size(axis)
    leading, last = (max(0, -steps), min(count, count - steps))
    return lax.ppermute(value, axis, [(source, source + steps) for source in range(leading, last)])


def nt(a, b):
    return lax.dot_general(a, b, (((1,), (1,)), ((), ())), preferred_element_type=jnp.float32)


def nn(a, b):
    return lax.dot_general(a, b, (((1,), (0,)), ((), ())), preferred_element_type=jnp.float32)


def starts_of(len_ref, first, count):
    docs = len_ref.shape[1]
    j = lax.broadcasted_iota(jnp.int32, (docs, docs), 0)
    k = lax.broadcasted_iota(jnp.int32, (docs, docs), 1)
    ends = jnp.sum(jnp.where(k <= j, len_ref[...], 0), axis=1, keepdims=True)
    lens = jnp.sum(jnp.where(k == j, len_ref[...], 0), axis=1, keepdims=True)
    pos = first + lax.broadcasted_iota(jnp.int32, (1, count), 1)
    return jnp.sum(jnp.where(ends <= pos, lens, 0), axis=0, keepdims=True)


def masked(plain, start, key_first, causal):
    sub = lax.broadcasted_iota(jnp.int32, plain.shape, 0)
    seen = sub >= start - key_first
    if causal:
        seen = seen & (sub <= lax.broadcasted_iota(jnp.int32, plain.shape, 1))
    return jnp.where(seen, plain * (SCALE * LOG2E), -1e30)


def softmax_kernel(shard_ref, len_ref, q_ref, kv0_ref, kv1_ref, kv2_ref, weight_ref, start_ref, lse_ref):
    rows = q_ref.shape[0]
    first = shard_ref[0] * rows
    start = starts_of(len_ref, first, rows)
    q = q_ref[...]
    scores = [
        masked(nt(kv[:rows], q), start, first - distance * rows, distance == 0)
        for distance, kv in enumerate((kv0_ref, kv1_ref, kv2_ref))
    ]
    highest = functools.reduce(jnp.maximum, [jnp.max(s, axis=0, keepdims=True) for s in scores])
    probs = [jnp.exp2(s - highest) for s in scores]
    total = functools.reduce(jnp.add, [jnp.sum(p, axis=0, keepdims=True) for p in probs])
    inverse = 1.0 / total
    start_ref[...] = start
    lse_ref[...] = highest + jnp.log2(total)
    for distance in range(SPAN + 1):
        weight_ref[distance] = (probs[distance] * inverse).astype(jnp.bfloat16)


def far_kernel(weight_ref, q_ref, do_ref, kv0_ref, kv1_ref, kv2_ref, one_ref, two_ref, delta_ref):
    rows = do_ref.shape[0]
    q = q_ref[...]
    do = do_ref[...]
    dprobs = [nt(kv[rows:], do) for kv in (kv0_ref, kv1_ref, kv2_ref)]
    weights = [weight_ref[distance] for distance in range(SPAN + 1)]
    delta = functools.reduce(
        jnp.add,
        [jnp.sum(w.astype(jnp.float32) * d, axis=0, keepdims=True) for w, d in zip(weights, dprobs)],
    )
    delta_ref[...] = delta
    for distance, out_ref in ((2, two_ref), (1, one_ref)):
        dscore = (weights[distance].astype(jnp.float32) * (dprobs[distance] - delta)).astype(jnp.bfloat16)
        out_ref[:rows] = nn(dscore, q).astype(jnp.bfloat16)
        out_ref[rows:] = nn(weights[distance], do).astype(jnp.bfloat16)


def own_kernel(shard_ref, start_ref, lse_ref, delta_ref, q_ref, do_ref, kv0_ref, kv1_ref, kv2_ref, dq_ref, own_ref):
    rows = q_ref.shape[0]
    first = shard_ref[0] * rows
    q = q_ref[...]
    do = do_ref[...]
    dq_t = jnp.zeros((DH, rows), jnp.float32)
    for distance, kv in enumerate((kv0_ref, kv1_ref, kv2_ref)):
        score = masked(nt(kv[:rows], q), start_ref[...], first - distance * rows, distance == 0)
        prob = jnp.exp2(score - lse_ref[...])
        dscore = (prob * (nt(kv[rows:], do) - delta_ref[...])).astype(jnp.bfloat16)
        dq_t = dq_t + nn(kv[:rows].T, dscore)
        if distance == 0:
            own_ref[:rows] = nn(dscore, q)
            own_ref[rows:] = nn(prob.astype(jnp.bfloat16), do)
    dq_ref[...] = (dq_t.T * SCALE).astype(dq_ref.dtype)


def sum_kernel(own_ref, two_ref, one_ref, out_ref):
    rows = own_ref.shape[0] // 2
    heads, _, part, _ = out_ref.shape
    total = own_ref[...] + one_ref[...].astype(jnp.float32) + two_ref[...].astype(jnp.float32)
    out_ref[:, 0] = (total[:rows] * SCALE).astype(jnp.bfloat16).reshape(heads, part, DH)
    out_ref[:, 1] = total[rows:].astype(jnp.bfloat16).reshape(heads, part, DH)


def call(kernel, name, out_shape, in_specs, tiles, *operands):
    return pl.pallas_call(
        kernel,
        out_shape=out_shape,
        in_specs=in_specs,
        out_specs=jax.tree.map(lambda _: VMEM, out_shape),
        compiler_params=pltpu.CompilerParams(vmem_limit_bytes=20 * 1024 * 1024),
        cost_estimate=pl.CostEstimate(
            flops=tiles * 2 * 512 * 512 * DH, bytes_accessed=1 << 20, transcendentals=tiles * 512 * 512
        ),
        name=name,
    )(*operands)


def shards(queries, keys, values, d_out, lengths):
    rows = keys.shape[0]
    heads = lax.axis_size("head")
    part = rows // heads
    docs = lengths.shape[0]
    shape = jax.ShapeDtypeStruct
    pair = (2 * rows, DH)
    zero = jnp.zeros((), keys.dtype)
    groups = part // 8
    tiles = d_out.reshape(groups, 8, heads, DH).transpose(0, 2, 1, 3).reshape(rows, DH)
    kv = lax.pad(keys, zero, ((0, rows, 0), (0, 0, 0))) + lax.pad(values, zero, ((rows, 0, 0), (0, 0, 0)))
    by_head = tiles.reshape(groups, heads, 8, DH).transpose(1, 0, 2, 3).reshape(heads, part, DH)
    kv2 = shifted(kv, "ctx", 2)
    kv1 = shifted(kv, "ctx", 1)
    do = lax.all_to_all(by_head, "head", split_axis=0, concat_axis=0, tiled=True).reshape(rows, DH)
    shard = lax.axis_index("ctx").astype(jnp.int32).reshape(1)
    weights, start, lse = call(
        softmax_kernel,
        "softmax",
        (
            shape((SPAN + 1, rows, rows), jnp.bfloat16),
            shape((1, rows), jnp.int32),
            shape((1, rows), jnp.float32),
        ),
        [SMEM] + [VMEM] * 5,
        6,
        shard, lengths.reshape(1, docs), queries, kv, kv1, kv2,
    )
    one, two, delta = call(
        far_kernel,
        "far",
        (shape(pair, jnp.bfloat16), shape(pair, jnp.bfloat16), shape((1, rows), jnp.float32)),
        [VMEM] * 6,
        7,
        weights, queries, do, kv, kv1, kv2,
    )
    two = shifted(two, "ctx", -2)
    one = shifted(one, "ctx", -1)
    grad_queries, own = call(
        own_kernel,
        "own",
        (shape((rows, DH), jnp.bfloat16), shape(pair, jnp.float32)),
        [SMEM] + [VMEM] * 8,
        11,
        shard, start, lse, delta, queries, do, kv, kv1, kv2,
    )
    total = call(sum_kernel, "total", shape((heads, 2, part, DH), jnp.bfloat16), [VMEM] * 3, 1, own, two, one)
    shares = lax.all_to_all(total, "head", split_axis=0, concat_axis=0, tiled=True)
    share = jnp.sum(shares.astype(jnp.float32), axis=0).astype(jnp.bfloat16)
    return (grad_queries, share[0][None], share[1][None])


def solution(mesh):
    in_specs = (P("ctx", "head"), P("ctx", None), P("ctx", None), P("ctx", "head", None), P())
    out_specs = (P("ctx", "head"), P("ctx", "head", None), P("ctx", "head", None))
    return jax.shard_map(shards, mesh=mesh, in_specs=in_specs, out_specs=out_specs, check_vma=False)
```

```python
import functools

import jax
import jax.numpy as jnp
from jax import lax
from jax.experimental import pallas as pl
from jax.experimental.pallas import tpu as pltpu
from jax.sharding import PartitionSpec as P

DH = 128
SPAN = 2
LOG2E = 1.4426950408889634
SCALE = DH ** (-0.5)
VMEM = pl.BlockSpec(memory_space=pltpu.VMEM)
SMEM = pl.BlockSpec(memory_space=pltpu.SMEM)


def shifted(value, axis, steps):
    count = lax.axis_size(axis)
    leading, last = (max(0, -steps), min(count, count - steps))
    return lax.ppermute(value, axis, [(source, source + steps) for source in range(leading, last)])


def nt(a, b):
    return lax.dot_general(a, b, (((1,), (1,)), ((), ())), preferred_element_type=jnp.float32)


def nn(a, b):
    return lax.dot_general(a, b, (((1,), (0,)), ((), ())), preferred_element_type=jnp.float32)


def starts_of(len_ref, first, count):
    docs = len_ref.shape[1]
    j = lax.broadcasted_iota(jnp.int32, (docs, docs), 0)
    k = lax.broadcasted_iota(jnp.int32, (docs, docs), 1)
    ends = jnp.sum(jnp.where(k <= j, len_ref[...], 0), axis=1, keepdims=True)
    lens = jnp.sum(jnp.where(k == j, len_ref[...], 0), axis=1, keepdims=True)
    pos = first + lax.broadcasted_iota(jnp.int32, (1, count), 1)
    return jnp.sum(jnp.where(ends <= pos, lens, 0), axis=0, keepdims=True)


def masked(plain, start, key_first, causal):
    sub = lax.broadcasted_iota(jnp.int32, plain.shape, 0)
    seen = sub >= start - key_first
    if causal:
        seen = seen & (sub <= lax.broadcasted_iota(jnp.int32, plain.shape, 1))
    return jnp.where(seen, plain * (SCALE * LOG2E), -1e30)


def load_kernel(shard_ref, len_ref, q_ref, start_ref, out_ref):
    rows = q_ref.shape[0]
    start_ref[...] = starts_of(len_ref, shard_ref[0] * rows, rows)
    out_ref[...] = q_ref[...]


def softmax_kernel(shard_ref, start_ref, q_ref, kv0_ref, kv1_ref, kv2_ref, weight_ref, lse_ref):
    rows = q_ref.shape[0]
    first = shard_ref[0] * rows
    start = start_ref[...]
    q = q_ref[...]
    scores = [
        masked(nt(kv[:rows], q), start, first - distance * rows, distance == 0)
        for distance, kv in enumerate((kv0_ref, kv1_ref, kv2_ref))
    ]
    highest = functools.reduce(jnp.maximum, [jnp.max(s, axis=0, keepdims=True) for s in scores])
    probs = [jnp.exp2(s - highest) for s in scores]
    total = functools.reduce(jnp.add, [jnp.sum(p, axis=0, keepdims=True) for p in probs])
    inverse = 1.0 / total
    lse_ref[...] = highest + jnp.log2(total)
    for distance in range(SPAN + 1):
        weight_ref[distance] = (probs[distance] * inverse).astype(jnp.bfloat16)


def far_kernel(shard_ref, start_ref, weight_ref, q_ref, do_ref, kv0_ref, kv1_ref, kv2_ref,
               one_ref, two_ref, delta_ref):
    rows = do_ref.shape[0]
    q = q_ref[...]
    do = do_ref[...]
    half = rows // 2
    reach = (shard_ref[0] - 1) * rows - jnp.min(start_ref[...])
    near = nt(kv1_ref[rows:], do)
    delta_ref[...] = jnp.sum(
        weight_ref[0].astype(jnp.float32) * nt(kv0_ref[rows:], do), axis=0, keepdims=True
    ) + jnp.sum(weight_ref[1].astype(jnp.float32) * near, axis=0, keepdims=True)

    def farthest(keys_at, count):
        weight = weight_ref[2, keys_at:, :count]
        dprob = nt(kv2_ref[rows + keys_at :], do[:count])
        delta = delta_ref[:, :count] + jnp.sum(weight.astype(jnp.float32) * dprob, axis=0, keepdims=True)
        delta_ref[:, :count] = delta
        dscore = (weight.astype(jnp.float32) * (dprob - delta)).astype(jnp.bfloat16)
        two_ref[keys_at:rows] = nn(dscore, q[:count]).astype(jnp.bfloat16)
        two_ref[rows + keys_at :] = nn(weight, do[:count]).astype(jnp.bfloat16)

    @pl.when((reach > 0) & (reach <= half))
    def _():
        two_ref[:half] = jnp.zeros((half, DH), jnp.bfloat16)
        two_ref[rows : rows + half] = jnp.zeros((half, DH), jnp.bfloat16)
        farthest(half, rows)

    @pl.when(reach > half)
    def _():
        farthest(0, half)

    @pl.when(reach <= 0)
    def _():
        two_ref[...] = jnp.zeros_like(two_ref)

    dscore = (weight_ref[1].astype(jnp.float32) * (near - delta_ref[...])).astype(jnp.bfloat16)
    one_ref[:rows] = nn(dscore, q).astype(jnp.bfloat16)
    one_ref[rows:] = nn(weight_ref[1], do).astype(jnp.bfloat16)


def own_kernel(shard_ref, start_ref, lse_ref, delta_ref, q_ref, do_ref, kv0_ref, kv1_ref, kv2_ref, dq_ref, own_ref):
    rows = q_ref.shape[0]
    first = shard_ref[0] * rows
    q = q_ref[...]
    do = do_ref[...]
    dq_t = jnp.zeros((DH, rows), jnp.float32)
    for distance, kv in enumerate((kv0_ref, kv1_ref, kv2_ref)):
        score = masked(nt(kv[:rows], q), start_ref[...], first - distance * rows, distance == 0)
        prob = jnp.exp2(score - lse_ref[...])
        dscore = (prob * (nt(kv[rows:], do) - delta_ref[...])).astype(jnp.bfloat16)
        dq_t = dq_t + nn(kv[:rows].T, dscore)
        if distance == 0:
            own_ref[:rows] = nn(dscore, q)
            own_ref[rows:] = nn(prob.astype(jnp.bfloat16), do)
    dq_ref[...] = (dq_t.T * SCALE).astype(dq_ref.dtype)


def sum_kernel(own_ref, two_ref, one_ref, out_ref):
    rows = own_ref.shape[0] // 2
    heads, _, part, _ = out_ref.shape
    total = own_ref[...] + one_ref[...].astype(jnp.float32) + two_ref[...].astype(jnp.float32)
    out_ref[:, 0] = (total[:rows] * SCALE).astype(jnp.bfloat16).reshape(heads, part, DH)
    out_ref[:, 1] = total[rows:].astype(jnp.bfloat16).reshape(heads, part, DH)


def call(kernel, name, out_shape, in_specs, tiles, *operands, scratch=()):
    return pl.pallas_call(
        kernel,
        out_shape=out_shape,
        in_specs=in_specs,
        out_specs=jax.tree.map(lambda _: VMEM, out_shape),
        scratch_shapes=scratch,
        compiler_params=pltpu.CompilerParams(vmem_limit_bytes=20 * 1024 * 1024),
        cost_estimate=pl.CostEstimate(
            flops=tiles * 2 * 512 * 512 * DH, bytes_accessed=1 << 20, transcendentals=tiles * 512 * 512
        ),
        name=name,
    )(*operands)


def shards(queries, keys, values, d_out, lengths):
    rows = keys.shape[0]
    heads = lax.axis_size("head")
    part = rows // heads
    docs = lengths.shape[0]
    shape = jax.ShapeDtypeStruct
    pair = (2 * rows, DH)
    zero = jnp.zeros((), keys.dtype)
    groups = part // 8
    tiles = d_out.reshape(groups, 8, heads, DH).transpose(0, 2, 1, 3).reshape(rows, DH)
    kv = lax.pad(keys, zero, ((0, rows, 0), (0, 0, 0))) + lax.pad(values, zero, ((rows, 0, 0), (0, 0, 0)))
    by_head = tiles.reshape(groups, heads, 8, DH).transpose(1, 0, 2, 3).reshape(heads, part, DH)
    kv2 = shifted(kv, "ctx", 2)
    kv1 = shifted(kv, "ctx", 1)
    do = lax.all_to_all(by_head, "head", split_axis=0, concat_axis=0, tiled=True).reshape(rows, DH)
    shard = lax.axis_index("ctx").astype(jnp.int32).reshape(1)
    start, queries = call(
        load_kernel,
        "load",
        (shape((1, rows), jnp.int32), shape((rows, DH), jnp.bfloat16)),
        [SMEM] + [VMEM] * 2,
        1,
        shard, lengths.reshape(1, docs), queries,
    )
    weights, lse = call(
        softmax_kernel,
        "softmax",
        (
            shape((SPAN + 1, rows, rows), jnp.bfloat16),
            shape((1, rows), jnp.float32),
        ),
        [SMEM] + [VMEM] * 5,
        6,
        shard, start, queries, kv, kv1, kv2,
    )
    one, two, delta = call(
        far_kernel,
        "far",
        (shape(pair, jnp.bfloat16), shape(pair, jnp.bfloat16), shape((1, rows), jnp.float32)),
        [SMEM] + [VMEM] * 7,
        7,
        shard, start, weights, queries, do, kv, kv1, kv2,
    )
    two = shifted(two, "ctx", -2)
    one = shifted(one, "ctx", -1)
    grad_queries, own = call(
        own_kernel,
        "own",
        (shape((rows, DH), jnp.bfloat16), shape(pair, jnp.float32)),
        [SMEM] + [VMEM] * 8,
        11,
        shard, start, lse, delta, queries, do, kv, kv1, kv2,
    )
    total = call(sum_kernel, "total", shape((heads, 2, part, DH), jnp.bfloat16), [VMEM] * 3, 1, own, two, one)
    shares = lax.all_to_all(total, "head", split_axis=0, concat_axis=0, tiled=True)
    share = jnp.sum(shares.astype(jnp.float32), axis=0).astype(jnp.bfloat16)
    return (grad_queries, share[0][None], share[1][None])


def solution(mesh):
    in_specs = (P("ctx", "head"), P("ctx", None), P("ctx", None), P("ctx", "head", None), P())
    out_specs = (P("ctx", "head"), P("ctx", "head", None), P("ctx", "head", None))
    return jax.shard_map(shards, mesh=mesh, in_specs=in_specs, out_specs=out_specs, check_vma=False)
```
